256 devices in a mesh: dp: 4 (over y_hi, core), ctx: 64 (over y_lo, x, z).
Axes of the slice: x: 4, y: 4 (y_hi: 2, y_lo: 2; y = y_hi * 2 + y_lo), z: 8, core: 2. Of those that a mesh axis runs over, the one named last changes fastest.
Arguments:
- queries: bfloat16 [65536, 1024], P(('dp', 'ctx')), parts along dimension 0, may hold values from -128 to 128
- keys: bfloat16 [65536, 128], P(('dp', 'ctx')), parts along dimension 0, may hold values from -4.1 to 4.1
- values: bfloat16 [65536, 128], P(('dp', 'ctx')), parts along dimension 0, may hold values from -6 to 6
- positions: int32 [65536], P(('dp', 'ctx')), parts along dimension 0, may hold values from 0 to 16383, as said below
- valid_length: int32 [4], P('dp'), parts along dimension 0, may hold values from 8192 to 16384
Outputs:
- attended: bfloat16 [65536, 1024], P(('dp', 'ctx')), parts along dimension 0
- log_sum_exp: float32 [8, 65536], P(None, ('dp', 'ctx')), parts along dimension 1
The draws below stay inside these ranges and needn't reach their ends.
There are 4 independent parts, one for each index of `dp`. The reference program is written for one: setup_inputs(seed, part) draws one part's arguments, and reference() takes and returns one part's arrays. A program takes and returns all parts, laid end to end along the dimension named above; each array names one. Nothing has to cross between parts.
Inputs may be any that keep to these rules, and one draw needn't show every extreme that they name: One sequence's positions are a permutation of its token indices made of aligned runs of 128 consecutive values; each device holds whole runs, in pairs whose first positions sum to 16256.
All inputs are finite; a program needn't handle non-finite values.
Results may differ from the reference program's by a relative error of at most 0.0075.
Values may be sent and summed in bfloat16 or wider, within the bound.
No kernel may reach another device: no remote copies, remote signals or barrier semaphores. Data moves between devices by JAX's collectives and lax.ppermute only.
A program may use at most 64 MiB of HBM per device.

```python
import jax
import jax.numpy as jnp
from jax import lax

H = 8
DH = 128
T_DEV = 256
SPAN = 128
TOKENS = 16384


def span_positions(key):
    pairs = TOKENS // (2 * SPAN)
    order = jax.random.permutation(jax.random.fold_in(key, 21), pairs)
    flip = jax.random.randint(jax.random.fold_in(key, 22), (pairs,), 0, 2)
    first = jnp.where(flip == 1, 2 * pairs - 1 - order, order)
    second = 2 * pairs - 1 - first
    span_ids = jnp.stack([first, second], axis=1).reshape(-1)
    inner = jnp.arange(SPAN, dtype=jnp.int32)
    return (span_ids[:, None] * SPAN + inner[None, :]).reshape(TOKENS).astype(jnp.int32)


def shared_keys(key):
    raw = jnp.clip(jax.random.normal(jax.random.fold_in(key, 23), (TOKENS, DH), jnp.float32), -4.0, 4.0)
    return raw


def draw_positions(key, part):
    placed = span_positions(key)
    return placed


def draw_keys(key, part):
    raw = shared_keys(key)
    return raw.astype(jnp.bfloat16)


def draw_queries(key, part):
    key = jax.random.fold_in(key, 3)
    base = jnp.clip(jax.random.normal(key, (TOKENS, H, DH), jnp.float32), -4.0, 4.0)
    return base.reshape(TOKENS, H * DH).astype(jnp.bfloat16)


def block_scale(stream_key, shape, shards, low, top_value):
    gain, own = 1.0, jax.random.fold_in(stream_key, 6)
    for dim, shards_of in shards:
        draws = jnp.exp(jax.random.uniform(jax.random.fold_in(own, dim), (shards_of,), jnp.float32, low / len(shards), top_value / len(shards)))
        gain = gain * jnp.repeat(draws, shape[dim] // shards_of).reshape([-1 if axis == dim else 1 for axis in range(len(shape))])
    return gain


def noise(key, dims, scale, reach, split=(), kind=jnp.bfloat16):
    result = jax.random.normal(key, dims, jnp.float32) * scale
    if len(split) > 0:
        result = block_scale(key, dims, split, -0.22, 0.18) * result
    return jnp.clip(result, min=-reach, max=reach).astype(kind)


def setup_inputs(seed: int = 0, part: int = 0) -> dict:
    key_list = jax.random.split(jax.random.key(seed), 6)
    own_keys = jax.random.split(jax.random.fold_in(key_list[5], part), 6)
    return {
        "queries": draw_queries(jax.random.fold_in(jax.random.fold_in(key_list[5], part), 71), part),
        "keys": draw_keys(jax.random.fold_in(jax.random.fold_in(key_list[5], part), 71), part),
        "values": noise(own_keys[2], (TOKENS, DH), 1.0, 6.0, ((0, 64),)),
        "positions": draw_positions(jax.random.fold_in(jax.random.fold_in(key_list[5], part), 71), part),
        "valid_length": jax.random.randint(own_keys[4], (1,), TOKENS // 2, TOKENS + 1).astype(jnp.int32),
    }


def reference(queries, keys, values, positions, valid_length):
    scale = 1.0 / (DH ** 0.5)
    length = valid_length[0]
    key_ok = positions < length
    blocks = TOKENS // T_DEV
    query_blocks = queries.reshape(blocks, T_DEV, H, DH)
    pos_blocks = positions.reshape(blocks, T_DEV)
    keys_wide = keys.astype(jnp.float32)
    values_wide = values.astype(jnp.float32)

    def one_block(pair):
        block_q, block_pos = pair
        scores = jnp.einsum('thd,kd->htk', block_q.astype(jnp.float32), keys_wide) * scale
        visible = (positions[None, :] <= block_pos[:, None]) & key_ok[None, :]
        scores = jnp.where(visible[None], scores, -jnp.inf)
        row_max = jnp.max(scores, axis=-1)
        expo = jnp.where(visible[None], jnp.exp(scores - row_max[..., None]), 0.0)
        total = jnp.sum(expo, axis=-1)
        weights = expo.astype(jnp.bfloat16)
        mixed = jnp.einsum('htk,kd->thd', weights.astype(jnp.float32), values_wide)
        mixed = mixed / jnp.transpose(total)[:, :, None]
        return mixed.astype(jnp.bfloat16), row_max + jnp.log(total)

    outs, lses = lax.map(one_block, (query_blocks, pos_blocks))
    attended = outs.reshape(TOKENS, H * DH)
    log_sum_exp = jnp.transpose(lses, (1, 0, 2)).reshape(H, TOKENS)
    return attended, log_sum_exp
```

```python
import functools
import math

import jax
import jax.numpy as jnp
from jax import lax
from jax.experimental import pallas as pl
from jax.experimental.pallas import tpu as pltpu
from jax.sharding import PartitionSpec as P

SPAN = 128
HEADS = 8
DEPTH = 128
ROWS = HEADS * SPAN
BLOCK = 4 * SPAN + 16
QROWS = 2 * SPAN + 16
ACC = DEPTH + 16
TILE = 256
TILES = ROWS // TILE
LAST = 127
UNITS = math.log2(math.e) / math.sqrt(DEPTH)
SCALE = 1.0 / math.sqrt(DEPTH)
EMPTY = -1e20
HIDDEN = -1e30
OPEN = -(1 << 20)
SHUT = 1 << 20
Y, X, Z = 2, 4, 8

f32 = jnp.float32
bf16 = jnp.bfloat16
VMEM = pl.BlockSpec(memory_space=pltpu.VMEM)
SMEM = pl.BlockSpec(memory_space=pltpu.SMEM)
ANY = pl.BlockSpec(memory_space=pl.ANY)
PARAMS = pltpu.CompilerParams(vmem_limit_bytes=48 * 2**20)


def low_rows(pos_ref):
    first, second = pos_ref[0], pos_ref[SPAN]
    return (
        pl.multiple_of(jnp.where(first < second, 0, SPAN), SPAN),
        pl.multiple_of(jnp.where(first < second, SPAN, 0), SPAN),
        lax.shift_right_logical(jnp.minimum(first, second), 7),
    )


def pack_kv_kernel(pos_ref, k_ref, v_ref, out_ref):
    low, high, run = low_rows(pos_ref)
    for i, start in enumerate((low, high)):
        out_ref[i * SPAN : (i + 1) * SPAN, :] = k_ref[pl.ds(start, SPAN), :]
        out_ref[(2 + i) * SPAN : (3 + i) * SPAN, :] = v_ref[pl.ds(start, SPAN), :].T
    out_ref[4 * SPAN :, :] = jnp.full((16, DEPTH), run.astype(f32), f32).astype(bf16)


def pack_q_kernel(pos_ref, q_ref, out_ref):
    low, high, run = low_rows(pos_ref)
    for i, start in enumerate((low, high)):
        for h in range(HEADS):
            cols = slice(h * SPAN, (h + 1) * SPAN)
            out_ref[i * SPAN : (i + 1) * SPAN, cols] = q_ref[pl.ds(start, SPAN), cols].T
    out_ref[2 * SPAN :, :] = jnp.full((16, ROWS), run.astype(f32), f32).astype(bf16)


def run_of(tile):
    return jnp.max(tile.astype(f32)).astype(jnp.int32)


def attend(sizes, pairs, refs, len_ref, qt, kv, o_ref, m_ref, s_ref, addr, base, slot_of, sems, more=()):
    q_refs, kv_refs = refs[:pairs], refs[pairs:]
    copies = []
    for i, (source, target) in enumerate(more):
        copies.append(pltpu.make_async_copy(source, target, sems.at[pairs + len(sizes) + i]))
    for i, ref in enumerate(q_refs):
        copies.append(pltpu.make_async_copy(ref, qt.at[i], sems.at[i]))
    at = 0
    for i, (ref, blocks) in enumerate(zip(kv_refs, sizes)):
        copies.append(
            pltpu.make_async_copy(ref, kv.at[pl.ds(at * BLOCK, blocks * BLOCK)], sems.at[pairs + i])
        )
        at += blocks
    total = at
    for c in copies:
        c.start()
    for c in copies:
        c.wait()

    length = len_ref[0]
    runs_q = [run_of(qt[i, 2 * SPAN : 2 * SPAN + 16, :DEPTH]) for i in range(pairs)]
    runs_k = [run_of(kv[b * BLOCK + 4 * SPAN : (b + 1) * BLOCK, :]) for b in range(total)]

    count = jnp.int32(0)

    def append(count, slot, row, first, wanted):
        addr[count] = row
        base[count] = first
        slot_of[lax.shift_right_logical(count, 1)] = slot
        return count + wanted.astype(jnp.int32)

    def pad(count, slot):
        return append(count, slot, 0, SHUT, (count & 1) == 1)

    for i in range(pairs):
        mine = runs_q[i]
        for b in range(total):
            r = runs_k[b]
            count = append(
                count, 2 * i, b * BLOCK, jnp.where(r < mine, OPEN, r * SPAN), r <= mine
            )
        count = pad(count, 2 * i)
        for b in range(total):
            count = append(count, 2 * i + 1, b * BLOCK, OPEN, jnp.bool_(True))
        for b in range(total):
            r = runs_k[b]
            first = (LAST - r) * SPAN
            full = (r > mine) & (first + SPAN <= length)
            count = append(
                count,
                2 * i + 1,
                b * BLOCK + SPAN,
                jnp.where(full, OPEN, first),
                (r >= mine) & (first < length),
            )
        count = pad(count, 2 * i + 1)
    items = lax.shift_right_logical(count, 1)

    ones = jnp.ones((16, 2 * SPAN), bf16)
    lane = lax.broadcasted_iota(jnp.int32, (1, TILE), 1) & (SPAN - 1)
    row = lax.broadcasted_iota(jnp.int32, (SPAN, 1), 0)

    def keys_at(i):
        a = pl.multiple_of(addr[2 * i], 16)
        b = pl.multiple_of(addr[2 * i + 1], 16)
        return jnp.concatenate([kv[pl.ds(a, SPAN), :], kv[pl.ds(b, SPAN), :]], 0)

    def values_at(i):
        a = pl.multiple_of(addr[2 * i] + 2 * SPAN, 16)
        b = pl.multiple_of(addr[2 * i + 1] + 2 * SPAN, 16)
        both = jnp.concatenate([kv[pl.ds(a, SPAN), :], kv[pl.ds(b, SPAN), :]], 1)
        return jnp.concatenate([both, ones], 0)

    def scores(i, t, keys):
        s = slot_of[i]
        q = qt[
            lax.shift_right_logical(s, 1),
            pl.ds(pl.multiple_of((s & 1) * SPAN, SPAN), SPAN),
            t * TILE : (t + 1) * TILE,
        ]
        return jnp.dot(keys, q, preferred_element_type=f32)

    def visit(i, cur, masked):
        slot = slot_of[i]
        values = values_at(i)
        after = jnp.minimum(i + 1, items - 1)
        keys = keys_at(after)
        if masked:
            pair = lax.shift_right_logical(slot, 1)
            mine = runs_q[0] if pairs == 1 else jnp.where(pair == 0, runs_q[0], runs_q[1])
            mine = jnp.where((slot & 1) == 1, LAST - mine, mine)
            limit = jnp.minimum(mine * SPAN + lane, length - 1)
            spots = jnp.concatenate([base[2 * i] + row, base[2 * i + 1] + row], 0)

        def weigh(t):
            s = s_ref[cur, t]
            s_ref[1 - cur, t] = scores(after, t, keys)
            if masked:
                s = jnp.where(spots <= limit, s, HIDDEN)
            cols = slice(t * TILE, (t + 1) * TILE)
            old = m_ref[slot, :, cols]
            new = jnp.maximum(old, jnp.max(s, axis=0, keepdims=True))
            m_ref[slot, :, cols] = new
            return jnp.exp2(s * UNITS - new * UNITS).astype(bf16), jnp.exp2((old - new) * UNITS)

        def gather(t, weights, factor):
            cols = slice(t * TILE, (t + 1) * TILE)
            o_ref[slot, :, cols] = o_ref[slot, :, cols] * factor + jnp.dot(
                values, weights, preferred_element_type=f32
            )

        held = None
        for t in range(TILES):
            now = weigh(t)
            if held is not None:
                gather(t - 1, *held)
            held = now
        gather(TILES - 1, *held)

    def either(i, cur):
        masked = (base[2 * i] != OPEN) | (base[2 * i + 1] != OPEN)
        pl.when(masked)(lambda: visit(i, cur, True))
        pl.when(jnp.logical_not(masked))(lambda: visit(i, cur, False))

    keys = keys_at(0)
    for t in range(TILES):
        s_ref[0, t] = scores(0, t, keys)

    def step(i, _):
        either(2 * i, 0)
        pl.when(2 * i + 1 < items)(lambda: either(2 * i + 1, 1))
        return 0

    lax.fori_loop(0, lax.shift_right_logical(items + 1, 1), step, 0)


def scratch(sizes, pairs):
    total = sum(sizes)
    room = pairs * (3 * total + 4) + 2
    return [
        pltpu.VMEM((pairs, QROWS, ROWS), bf16),
        pltpu.VMEM((total * BLOCK, DEPTH), bf16),
        pltpu.VMEM((2, TILES, 2 * SPAN, TILE), f32),
        pltpu.SMEM((room,), jnp.int32),
        pltpu.SMEM((room,), jnp.int32),
        pltpu.SMEM((room,), jnp.int32),
        pltpu.SemaphoreType.DMA((pairs + len(sizes) + 2,)),
    ]


def first_kernel(sizes, pairs, len_ref, *refs):
    given = refs[: pairs + len(sizes)]
    o_ref, m_ref, qt, kv, s_ref, addr, base, slot_of, sems = refs[pairs + len(sizes) :]
    o_ref[...] = jnp.zeros_like(o_ref)
    m_ref[...] = jnp.full_like(m_ref, EMPTY)
    attend(sizes, pairs, given, len_ref, qt, kv, o_ref, m_ref, s_ref, addr, base, slot_of, sems)


def next_kernel(sizes, pairs, len_ref, *refs):
    given = refs[: pairs + len(sizes)]
    _, _, o_ref, m_ref, qt, kv, s_ref, addr, base, slot_of, sems = refs[pairs + len(sizes) :]
    attend(sizes, pairs, given, len_ref, qt, kv, o_ref, m_ref, s_ref, addr, base, slot_of, sems)


def normal(o_ref, m_ref, slot):
    total = o_ref[slot, DEPTH : DEPTH + 1, :]
    seen = total > 0.0
    safe = jnp.where(seen, total, 1.0)
    lse = jnp.where(seen, m_ref[slot] * SCALE + jnp.log(safe), HIDDEN)
    return o_ref[slot, :DEPTH, :] * (1.0 / safe), lse


def parcel_kernel(sizes, len_ref, *refs):
    given = refs[: 1 + len(sizes)]
    o_in, m_in, out_ref, o_ref, m_ref, qt, kv, s_ref, addr, base, slot_of, sems = refs[1 + len(sizes) :]
    more = ((o_in.at[pl.ds(0, 2)], o_ref), (m_in.at[pl.ds(0, 2)], m_ref))
    attend(
        sizes, 1, given, len_ref, qt, kv, o_ref, m_ref, s_ref, addr, base, slot_of, sems, more
    )
    place = lax.broadcasted_iota(jnp.int32, (16, ROWS), 0)
    extra = jnp.zeros((16, ROWS), f32)
    for slot in range(2):
        mixed, lse = normal(o_ref, m_ref, slot)
        out_ref[slot * SPAN : (slot + 1) * SPAN, :] = mixed.astype(bf16)
        for part in range(3):
            piece = lse.astype(bf16).astype(f32)
            extra = jnp.where(place == 3 * slot + part, piece, extra)
            lse = lse - piece
    out_ref[2 * SPAN :, :] = extra.astype(bf16)


def merge_kernel(pos_ref, o_ref, m_ref, theirs_ref, out_ref, lse_ref):
    low, high, _ = low_rows(pos_ref)
    extra = theirs_ref[2 * SPAN :, :].astype(f32)
    for slot, start in enumerate((low, high)):
        mixed, lse = normal(o_ref, m_ref, slot)
        other = extra[3 * slot : 3 * slot + 1] + extra[3 * slot + 1 : 3 * slot + 2]
        other = other + extra[3 * slot + 2 : 3 * slot + 3]
        top = jnp.maximum(lse, other)
        w_own, w_other = jnp.exp(lse - top), jnp.exp(other - top)
        total = w_own + w_other
        w_own, w_other = w_own / total, w_other / total
        both = top + jnp.log(total)
        for h in range(HEADS):
            cols = slice(h * SPAN, (h + 1) * SPAN)
            block = mixed[:, cols] * w_own[:, cols] + w_other[:, cols] * theirs_ref[
                slot * SPAN : (slot + 1) * SPAN, cols
            ].astype(f32)
            out_ref[pl.ds(start, SPAN), cols] = block.T.astype(bf16)
            lse_ref[h : h + 1, pl.ds(start, SPAN)] = both[:, cols]


def cost(blocks, pairs):
    work = blocks * pairs * 2 * ROWS * SPAN
    return pl.CostEstimate(
        flops=4 * DEPTH * work, bytes_accessed=blocks * BLOCK * DEPTH * 2, transcendentals=work
    )


def state_shape(slots):
    return (
        jax.ShapeDtypeStruct((slots, ACC, ROWS), f32),
        jax.ShapeDtypeStruct((slots, 1, ROWS), f32),
    )


def count_of(arrays):
    return tuple(a.shape[0] // BLOCK for a in arrays)


def first_visit(length, queries, blocks):
    sizes, pairs = count_of(blocks), len(queries)
    return pl.pallas_call(
        functools.partial(first_kernel, sizes, pairs),
        out_shape=state_shape(2 * pairs),
        in_specs=[SMEM] + [ANY] * (pairs + len(blocks)),
        out_specs=(VMEM, VMEM),
        scratch_shapes=scratch(sizes, pairs),
        compiler_params=PARAMS,
        cost_estimate=cost(sum(sizes), pairs),
        name="first_visit",
    )(length, *queries, *blocks)


def next_visit(length, queries, blocks, state):
    sizes, pairs = count_of(blocks), len(queries)
    at = 1 + pairs + len(blocks)
    return pl.pallas_call(
        functools.partial(next_kernel, sizes, pairs),
        out_shape=state_shape(2 * pairs),
        in_specs=[SMEM] + [ANY] * (pairs + len(blocks)) + [VMEM, VMEM],
        out_specs=(VMEM, VMEM),
        input_output_aliases={at: 0, at + 1: 1},
        scratch_shapes=scratch(sizes, pairs),
        compiler_params=PARAMS,
        cost_estimate=cost(sum(sizes), pairs),
        name="next_visit",
    )(length, *queries, *blocks, *state)


def parcel_visit(length, query, blocks, state):
    sizes = count_of(blocks)
    return pl.pallas_call(
        functools.partial(parcel_kernel, sizes),
        out_shape=jax.ShapeDtypeStruct((QROWS, ROWS), bf16),
        in_specs=[SMEM] + [ANY] * (1 + len(blocks)) + [ANY, ANY],
        out_specs=VMEM,
        scratch_shapes=[pltpu.VMEM((2, ACC, ROWS), f32), pltpu.VMEM((2, 1, ROWS), f32)]
        + scratch(sizes, 1),
        compiler_params=PARAMS,
        cost_estimate=cost(sum(sizes), 1),
        name="parcel_visit",
    )(length, query, *blocks, *state)


def own_kernel(sizes, len_ref, *refs):
    given = refs[: 1 + len(sizes)]
    o_in, m_in, o_ref, m_ref, qt, kv, s_ref, addr, base, slot_of, sems = refs[1 + len(sizes) :]
    more = ((o_in.at[pl.ds(2, 2)], o_ref), (m_in.at[pl.ds(2, 2)], m_ref))
    attend(
        sizes, 1, given, len_ref, qt, kv, o_ref, m_ref, s_ref, addr, base, slot_of, sems, more
    )


def own_visit(length, query, blocks, state):
    sizes = count_of(blocks)
    return pl.pallas_call(
        functools.partial(own_kernel, sizes),
        out_shape=state_shape(2),
        in_specs=[SMEM] + [ANY] * (1 + len(blocks)) + [ANY, ANY],
        out_specs=(VMEM, VMEM),
        scratch_shapes=scratch(sizes, 1),
        compiler_params=PARAMS,
        cost_estimate=cost(sum(sizes), 1),
        name="own_visit",
    )(length, query, *blocks, *state)


def place(y, x, z):
    return ((y % Y) * X + x % X) * Z + z % Z


def send(array, dy, dx, dz):
    pairs = [
        (place(y, x, z), place(y + dy, x + dx, z + dz))
        for y in range(Y)
        for x in range(X)
        for z in range(Z)
    ]
    return lax.ppermute(array, "ctx", pairs)


def shards(queries, keys, values, positions, valid_length):
    block = pl.pallas_call(
        pack_kv_kernel,
        out_shape=jax.ShapeDtypeStruct((BLOCK, DEPTH), bf16),
        in_specs=[SMEM, VMEM, VMEM],
        out_specs=VMEM,
        name="pack_kv",
    )(positions, keys, values)
    query = pl.pallas_call(
        pack_q_kernel,
        out_shape=jax.ShapeDtypeStruct((QROWS, ROWS), bf16),
        in_specs=[SMEM, VMEM],
        out_specs=VMEM,
        name="pack_q",
    )(positions, queries)

    near = [block, send(block, 0, 1, 0), send(block, 0, -1, 0), send(block, 0, 2, 0)]
    far = [send(block, 0, 0, 3), send(block, 0, 0, -3), send(block, 0, 0, 4)]
    theirs = send(query, 1, 0, 0)
    both = [theirs, query]

    row = jnp.concatenate(near, 0)
    up, down = send(row, 0, 0, 1), send(row, 0, 0, -1)
    state = first_visit(valid_length, both, [row])

    column = jnp.concatenate(far, 0)
    side = [send(column, 0, 1, 0), send(column, 0, -1, 0), send(column, 0, 2, 0)]
    up2, down2 = send(up, 0, 0, 1), send(down, 0, 0, -1)
    state = next_visit(valid_length, both, [column, up, down], state)

    late = side + [up2, down2]
    parcel = parcel_visit(valid_length, theirs, late, state)
    back = send(parcel, 1, 0, 0)
    own, own_max = own_visit(valid_length, query, late, state)
    return pl.pallas_call(
        merge_kernel,
        out_shape=(
            jax.ShapeDtypeStruct((2 * SPAN, ROWS), bf16),
            jax.ShapeDtypeStruct((HEADS, 2 * SPAN), f32),
        ),
        in_specs=[SMEM, VMEM, VMEM, VMEM],
        out_specs=(VMEM, VMEM),
        compiler_params=PARAMS,
        name="merge",
    )(positions, own, own_max, back)


def solution(mesh):
    placed = (
        P(("dp", "ctx"), None),
        P(("dp", "ctx"), None),
        P(("dp", "ctx"), None),
        P(("dp", "ctx")),
        P("dp"),
    )
    return jax.shard_map(
        shards,
        mesh=mesh,
        in_specs=placed,
        out_specs=(P(("dp", "ctx"), None), P(None, ("dp", "ctx"))),
        check_vma=False,
    )
```

```python
import functools
import math

import jax
import jax.numpy as jnp
from jax import lax
from jax.experimental import pallas as pl
from jax.experimental.pallas import tpu as pltpu
from jax.sharding import PartitionSpec as P

SPAN = 128
HEADS = 8
DEPTH = 128
ROWS = HEADS * SPAN
BLOCK = 4 * SPAN + 16
QROWS = 2 * SPAN + 16
ACC = DEPTH + 16
TILE = 256
TILES = ROWS // TILE
LAST = 127
UNITS = math.log2(math.e) / math.sqrt(DEPTH)
SCALE = 1.0 / math.sqrt(DEPTH)
EMPTY = -1e20
HIDDEN = -1e30
OPEN = -(1 << 20)
SHUT = 1 << 20
Y, X, Z = 2, 4, 8

f32 = jnp.float32
bf16 = jnp.bfloat16
VMEM = pl.BlockSpec(memory_space=pltpu.VMEM)
SMEM = pl.BlockSpec(memory_space=pltpu.SMEM)
ANY = pl.BlockSpec(memory_space=pl.ANY)
PARAMS = pltpu.CompilerParams(vmem_limit_bytes=48 * 2**20)


def low_rows(pos_ref):
    first, second = pos_ref[0], pos_ref[SPAN]
    return (
        pl.multiple_of(jnp.where(first < second, 0, SPAN), SPAN),
        pl.multiple_of(jnp.where(first < second, SPAN, 0), SPAN),
        lax.shift_right_logical(jnp.minimum(first, second), 7),
    )


def pack_kv_kernel(pos_ref, k_ref, v_ref, out_ref):
    low, high, run = low_rows(pos_ref)
    for i, start in enumerate((low, high)):
        out_ref[i * SPAN : (i + 1) * SPAN, :] = k_ref[pl.ds(start, SPAN), :]
        out_ref[(2 + i) * SPAN : (3 + i) * SPAN, :] = v_ref[pl.ds(start, SPAN), :].T
    out_ref[4 * SPAN :, :] = jnp.full((16, DEPTH), run.astype(f32), f32).astype(bf16)


def pack_q_kernel(pos_ref, q_ref, out_ref, copy_ref):
    low, high, run = low_rows(pos_ref)
    for i, start in enumerate((low, high)):
        for h in range(HEADS):
            cols = slice(h * SPAN, (h + 1) * SPAN)
            out_ref[i * SPAN : (i + 1) * SPAN, cols] = q_ref[pl.ds(start, SPAN), cols].T
    out_ref[2 * SPAN :, :] = jnp.full((16, ROWS), run.astype(f32), f32).astype(bf16)
    copy_ref[...] = out_ref[...]


def run_of(tile):
    return jnp.max(tile.astype(f32)).astype(jnp.int32)


def attend(sizes, kv_refs, kv, len_ref, q_ref, state, work, sems, fetch=True):
    o_ref, m_ref = state
    s_ref, addr, base, slot_of = work
    total = sum(sizes)
    if fetch and kv_refs is not None:
        copies = []
        at = 0
        for i, (ref, blocks) in enumerate(zip(kv_refs, sizes)):
            copies.append(
                pltpu.make_async_copy(ref, kv.at[pl.ds(at * BLOCK, blocks * BLOCK)], sems.at[i])
            )
            at += blocks
        for c in copies:
            c.start()
        for c in copies:
            c.wait()

    length = len_ref[0]
    mine = run_of(q_ref[2 * SPAN : 2 * SPAN + 16, :DEPTH])
    seen = range(total)
    runs = {b: run_of(kv[b * BLOCK + 4 * SPAN : (b + 1) * BLOCK, :]) for b in seen}

    def append(count, slot, row, first, wanted):
        addr[count] = row
        base[count] = first
        slot_of[lax.shift_right_logical(count, 1)] = slot
        return count + wanted.astype(jnp.int32)

    def pad(count, slot):
        return append(count, slot, 0, SHUT, (count & 1) == 1)

    count = jnp.int32(0)
    for b in seen:
        r = runs[b]
        count = append(count, 0, b * BLOCK, jnp.where(r < mine, OPEN, r * SPAN), r <= mine)
    count = pad(count, 0)
    for b in seen:
        count = append(count, 1, b * BLOCK, OPEN, jnp.bool_(True))
    for b in seen:
        r = runs[b]
        first = (LAST - r) * SPAN
        full = (r > mine) & (first + SPAN <= length)
        count = append(
            count,
            1,
            b * BLOCK + SPAN,
            jnp.where(full, OPEN, first),
            (r >= mine) & (first < length),
        )
    count = pad(count, 1)
    items = lax.shift_right_logical(count, 1)

    ones = jnp.ones((16, 2 * SPAN), bf16)
    lane = lax.broadcasted_iota(jnp.int32, (1, TILE), 1) & (SPAN - 1)
    row = lax.broadcasted_iota(jnp.int32, (SPAN, 1), 0)

    def keys_at(i):
        a = pl.multiple_of(addr[2 * i], 16)
        b = pl.multiple_of(addr[2 * i + 1], 16)
        return jnp.concatenate([kv[pl.ds(a, SPAN), :], kv[pl.ds(b, SPAN), :]], 0)

    def values_at(i):
        a = pl.multiple_of(addr[2 * i] + 2 * SPAN, 16)
        b = pl.multiple_of(addr[2 * i + 1] + 2 * SPAN, 16)
        both = jnp.concatenate([kv[pl.ds(a, SPAN), :], kv[pl.ds(b, SPAN), :]], 1)
        return jnp.concatenate([both, ones], 0)

    def scores(i, t, keys):
        start = pl.multiple_of(slot_of[i] * SPAN, SPAN)
        q = q_ref[pl.ds(start, SPAN), t * TILE : (t + 1) * TILE]
        return jnp.dot(keys, q, preferred_element_type=f32)

    def visit(i, cur, masked):
        slot = slot_of[i]
        values = values_at(i)
        after = jnp.minimum(i + 1, items - 1)
        keys = keys_at(after)
        if masked:
            run = jnp.where(slot == 1, LAST - mine, mine)
            limit = jnp.minimum(run * SPAN + lane, length - 1)
            spots = jnp.concatenate([base[2 * i] + row, base[2 * i + 1] + row], 0)

        def weigh(t):
            s = s_ref[cur, t]
            s_ref[1 - cur, t] = scores(after, t, keys)
            if masked:
                s = jnp.where(spots <= limit, s, HIDDEN)
            cols = slice(t * TILE, (t + 1) * TILE)
            old = m_ref[slot, :, cols]
            new = jnp.maximum(old, jnp.max(s, axis=0, keepdims=True))
            m_ref[slot, :, cols] = new
            return jnp.exp2(s * UNITS - new * UNITS).astype(bf16), jnp.exp2((old - new) * UNITS)

        def gather(t, weights, factor):
            cols = slice(t * TILE, (t + 1) * TILE)
            o_ref[slot, :, cols] = o_ref[slot, :, cols] * factor + jnp.dot(
                values, weights, preferred_element_type=f32
            )

        held = None
        for t in range(TILES):
            now = weigh(t)
            if held is not None:
                gather(t - 1, *held)
            held = now
        gather(TILES - 1, *held)

    def either(i, cur):
        masked = (base[2 * i] != OPEN) | (base[2 * i + 1] != OPEN)
        pl.when(masked)(lambda: visit(i, cur, True))
        pl.when(jnp.logical_not(masked))(lambda: visit(i, cur, False))

    keys = keys_at(0)
    for t in range(TILES):
        s_ref[0, t] = scores(0, t, keys)

    def step(i, _):
        either(2 * i, 0)
        pl.when(2 * i + 1 < items)(lambda: either(2 * i + 1, 1))
        return 0

    lax.fori_loop(0, lax.shift_right_logical(items + 1, 1), step, 0)


def scratch(sizes):
    total = sum(sizes)
    room = 3 * total + 6
    return [
        pltpu.VMEM((total * BLOCK, DEPTH), bf16),
        pltpu.SemaphoreType.DMA((len(sizes),)),
        pltpu.VMEM((2, TILES, 2 * SPAN, TILE), f32),
        pltpu.SMEM((room,), jnp.int32),
        pltpu.SMEM((room,), jnp.int32),
        pltpu.SMEM((room,), jnp.int32),
    ]


def blank(o_ref, m_ref):
    o_ref[...] = jnp.zeros_like(o_ref)
    m_ref[...] = jnp.full_like(m_ref, EMPTY)


def first_kernel(sizes, len_ref, q_ref, kv, o_ref, m_ref, s_ref, addr, base, slot_of):
    blank(o_ref, m_ref)
    work = (s_ref, addr, base, slot_of)
    attend(sizes, None, kv, len_ref, q_ref, (o_ref, m_ref), work, None)


def join_kernel(sizes, len_ref, q_ref, *refs):
    n = len(sizes)
    o_ref, m_ref, kv, sems, *work = refs[n:]
    blank(o_ref, m_ref)
    attend(sizes, refs[:n], kv, len_ref, q_ref, (o_ref, m_ref), work, sems)


def both_kernel(sizes, len_ref, theirs_ref, q_ref, *refs):
    n = len(sizes)
    _, _, _, _, o1, m1, o2, m2, kv, sems, *work = refs[n:]
    attend(sizes, refs[:n], kv, len_ref, theirs_ref, (o1, m1), work, sems)
    attend(sizes, refs[:n], kv, len_ref, q_ref, (o2, m2), work, sems, False)


def one_kernel(sizes, len_ref, q_ref, *refs):
    n = len(sizes)
    _, _, o_ref, m_ref, kv, sems, *work = refs[n:]
    attend(sizes, refs[:n], kv, len_ref, q_ref, (o_ref, m_ref), work, sems)


def normal(o_ref, m_ref, slot):
    total = o_ref[slot, DEPTH : DEPTH + 1, :]
    seen = total > 0.0
    safe = jnp.where(seen, total, 1.0)
    lse = jnp.where(seen, m_ref[slot] * SCALE + jnp.log(safe), HIDDEN)
    return o_ref[slot, :DEPTH, :] * (1.0 / safe), lse


def parcel_kernel(sizes, len_ref, q_ref, *refs):
    n = len(sizes)
    _, _, o_ref, m_ref, out_ref, kv, sems, *work = refs[n:]
    attend(sizes, refs[:n], kv, len_ref, q_ref, (o_ref, m_ref), work, sems)
    place = lax.broadcasted_iota(jnp.int32, (16, ROWS), 0)
    extra = jnp.zeros((16, ROWS), f32)
    for slot in range(2):
        mixed, lse = normal(o_ref, m_ref, slot)
        out_ref[slot * SPAN : (slot + 1) * SPAN, :] = mixed.astype(bf16)
        for part in range(3):
            piece = lse.astype(bf16).astype(f32)
            extra = jnp.where(place == 3 * slot + part, piece, extra)
            lse = lse - piece
    out_ref[2 * SPAN :, :] = extra.astype(bf16)


def merge_kernel(pos_ref, o_ref, m_ref, theirs_ref, out_ref, lse_ref):
    low, high, _ = low_rows(pos_ref)
    extra = theirs_ref[2 * SPAN :, :].astype(f32)
    for slot, start in enumerate((low, high)):
        mixed, lse = normal(o_ref, m_ref, slot)
        other = extra[3 * slot : 3 * slot + 1] + extra[3 * slot + 1 : 3 * slot + 2]
        other = other + extra[3 * slot + 2 : 3 * slot + 3]
        top = jnp.maximum(lse, other)
        w_own, w_other = jnp.exp(lse - top), jnp.exp(other - top)
        total = w_own + w_other
        w_own, w_other = w_own / total, w_other / total
        both = top + jnp.log(total)
        for h in range(HEADS):
            cols = slice(h * SPAN, (h + 1) * SPAN)
            block = mixed[:, cols] * w_own[:, cols] + w_other[:, cols] * theirs_ref[
                slot * SPAN : (slot + 1) * SPAN, cols
            ].astype(f32)
            out_ref[pl.ds(start, SPAN), cols] = block.T.astype(bf16)
            lse_ref[h : h + 1, pl.ds(start, SPAN)] = both[:, cols]


def cost(blocks, pairs):
    work = blocks * pairs * 2 * ROWS * SPAN
    return pl.CostEstimate(
        flops=20 * DEPTH * work, bytes_accessed=blocks * BLOCK * DEPTH * 2, transcendentals=work
    )


STATE = (
    jax.ShapeDtypeStruct((2, ACC, ROWS), f32),
    jax.ShapeDtypeStruct((2, 1, ROWS), f32),
)


def count_of(arrays):
    return tuple(a.shape[0] // BLOCK for a in arrays)


def visit(kernel, name, length, queries, blocks, given=(), shapes=STATE, pairs=None):
    sizes = count_of(blocks)
    at = 1 + len(queries) + len(blocks)
    alone = kernel is first_kernel
    spare = len(shapes) - len(given)
    shift = 0 if kernel is parcel_kernel else spare
    room = scratch(sizes)
    return pl.pallas_call(
        functools.partial(kernel, sizes),
        out_shape=shapes,
        in_specs=[SMEM] + [VMEM] * len(queries) + [VMEM if alone else ANY] * len(blocks) + [VMEM] * len(given),
        out_specs=(VMEM,) * len(shapes),
        input_output_aliases={at + i: shift + i for i in range(len(given))},
        scratch_shapes=room[2:] if alone else room,
        compiler_params=PARAMS,
        cost_estimate=cost(sum(sizes), pairs or len(queries)),
        name=name,
    )(length, *queries, *blocks, *given)


def place(y, x, z):
    return ((y % Y) * X + x % X) * Z + z % Z


def send(array, dy, dx, dz):
    pairs = [
        (place(y, x, z), place(y + dy, x + dx, z + dz))
        for y in range(Y)
        for x in range(X)
        for z in range(Z)
    ]
    return lax.ppermute(array, "ctx", pairs)


def shards(queries, keys, values, positions, valid_length):
    block = pl.pallas_call(
        pack_kv_kernel,
        out_shape=jax.ShapeDtypeStruct((BLOCK, DEPTH), bf16),
        in_specs=[SMEM, VMEM, VMEM],
        out_specs=VMEM,
        name="pack_kv",
    )(positions, keys, values)
    query, outgoing = pl.pallas_call(
        pack_q_kernel,
        out_shape=(pltpu.VMEM((QROWS, ROWS), bf16), jax.ShapeDtypeStruct((QROWS, ROWS), bf16)),
        in_specs=[SMEM, VMEM],
        out_specs=(VMEM, VMEM),
        name="pack_q",
    )(positions, queries)

    near = [block, send(block, 0, 1, 0), send(block, 0, -1, 0), send(block, 0, 2, 0)]
    far = [send(block, 0, 0, 4), send(block, 0, 0, 3), send(block, 0, 0, -3)]
    theirs = send(outgoing, 1, 0, 0)

    row = jnp.concatenate(near, 0)
    up, down = send(row, 0, 0, 1), send(row, 0, 0, -1)
    own = visit(first_kernel, "first_visit", valid_length, [query], [row])
    far, own = lax.optimization_barrier((far, own))
    column = jnp.concatenate(far, 0)
    side = [send(column, 0, 1, 0), send(column, 0, -1, 0), send(column, 0, 2, 0)]
    both = [theirs, query]
    other = visit(join_kernel, "join_visit", valid_length, [theirs], [row, column])
    up2, down2 = send(up, 0, 0, 1), send(down, 0, 0, -1)
    state = visit(
        both_kernel, "both_visit", valid_length, both, [up, down], (*other, *own), STATE + STATE
    )
    other = visit(one_kernel, "side_visit", valid_length, [theirs], side, state[:2])
    late = [up2, down2]
    packet = jax.ShapeDtypeStruct((QROWS, ROWS), bf16)
    parcel = visit(
        parcel_kernel, "parcel_visit", valid_length, [theirs], late, other, STATE + (packet,)
    )[2]
    back = send(parcel, 1, 0, 0)
    own, own_max = visit(one_kernel, "own_visit", valid_length, [query], [column] + side + late, state[2:])
    return pl.pallas_call(
        merge_kernel,
        out_shape=(
            jax.ShapeDtypeStruct((2 * SPAN, ROWS), bf16),
            jax.ShapeDtypeStruct((HEADS, 2 * SPAN), f32),
        ),
        in_specs=[SMEM, VMEM, VMEM, VMEM],
        out_specs=(VMEM, VMEM),
        compiler_params=PARAMS,
        name="merge",
    )(positions, own, own_max, back)


def solution(mesh):
    placed = (
        P(("dp", "ctx"), None),
        P(("dp", "ctx"), None),
        P(("dp", "ctx"), None),
        P(("dp", "ctx")),
        P("dp"),
    )
    return jax.shard_map(
        shards,
        mesh=mesh,
        in_specs=placed,
        out_specs=(P(("dp", "ctx"), None), P(None, ("dp", "ctx"))),
        check_vma=False,
    )
```

```python
import functools
import math

import jax
import jax.numpy as jnp
from jax import lax
from jax.experimental import pallas as pl
from jax.experimental.pallas import tpu as pltpu
from jax.sharding import PartitionSpec as P

SPAN = 128
HEADS = 8
DEPTH = 128
ROWS = HEADS * SPAN
BLOCK = 4 * SPAN + 16
QROWS = 2 * SPAN + 16
ACC = DEPTH + 16
TILE = 256
TILES = ROWS // TILE
LAST = 127
UNITS = math.log2(math.e) / math.sqrt(DEPTH)
SCALE = 1.0 / math.sqrt(DEPTH)
EMPTY = -1e20
HIDDEN = -1e30
OPEN = -(1 << 20)
SHUT = 1 << 20
Y, X, Z = 2, 4, 8

f32 = jnp.float32
bf16 = jnp.bfloat16
VMEM = pl.BlockSpec(memory_space=pltpu.VMEM)
SMEM = pl.BlockSpec(memory_space=pltpu.SMEM)
ANY = pl.BlockSpec(memory_space=pl.ANY)
PARAMS = pltpu.CompilerParams(vmem_limit_bytes=48 * 2**20)


def low_rows(pos_ref):
    first, second = pos_ref[0], pos_ref[SPAN]
    return (
        pl.multiple_of(jnp.where(first < second, 0, SPAN), SPAN),
        pl.multiple_of(jnp.where(first < second, SPAN, 0), SPAN),
        lax.shift_right_logical(jnp.minimum(first, second), 7),
    )


def pack_kv_kernel(pos_ref, k_ref, v_ref, out_ref):
    low, high, run = low_rows(pos_ref)
    for i, start in enumerate((low, high)):
        out_ref[i * SPAN : (i + 1) * SPAN, :] = k_ref[pl.ds(start, SPAN), :]
        out_ref[(2 + i) * SPAN : (3 + i) * SPAN, :] = v_ref[pl.ds(start, SPAN), :].T
    out_ref[4 * SPAN :, :] = jnp.full((16, DEPTH), run.astype(f32), f32).astype(bf16)


def pack_q_kernel(pos_ref, q_ref, out_ref, copy_ref):
    low, high, run = low_rows(pos_ref)
    for i, start in enumerate((low, high)):
        for h in range(HEADS):
            cols = slice(h * SPAN, (h + 1) * SPAN)
            out_ref[i * SPAN : (i + 1) * SPAN, cols] = q_ref[pl.ds(start, SPAN), cols].T
    out_ref[2 * SPAN :, :] = jnp.full((16, ROWS), run.astype(f32), f32).astype(bf16)
    copy_ref[...] = out_ref[...]


def run_of(tile):
    return jnp.max(tile.astype(f32)).astype(jnp.int32)


def attend(sizes, kv_refs, kv, len_ref, q_ref, state, work, sems, fetch=True, since=0):
    o_ref, m_ref = state
    s_ref, addr, base, slot_of = work
    total = sum(sizes)
    if fetch and kv_refs is not None:
        copies = []
        at = 0
        for i, (ref, blocks) in enumerate(zip(kv_refs, sizes)):
            copies.append(
                pltpu.make_async_copy(ref, kv.at[pl.ds(at * BLOCK, blocks * BLOCK)], sems.at[i])
            )
            at += blocks
        for c in copies:
            c.start()
        for c in copies:
            c.wait()

    length = len_ref[0]
    mine = run_of(q_ref[2 * SPAN : 2 * SPAN + 16, :DEPTH])
    seen = range(since, total)
    runs = {b: run_of(kv[b * BLOCK + 4 * SPAN : (b + 1) * BLOCK, :]) for b in seen}

    def append(count, slot, row, first, wanted):
        addr[count] = row
        base[count] = first
        slot_of[lax.shift_right_logical(count, 1)] = slot
        return count + wanted.astype(jnp.int32)

    def pad(count, slot):
        return append(count, slot, since * BLOCK, SHUT, (count & 1) == 1)

    count = jnp.int32(0)
    for b in seen:
        r = runs[b]
        count = append(count, 0, b * BLOCK, jnp.where(r < mine, OPEN, r * SPAN), r <= mine)
    count = pad(count, 0)
    for b in seen:
        count = append(count, 1, b * BLOCK, OPEN, jnp.bool_(True))
    for b in seen:
        r = runs[b]
        first = (LAST - r) * SPAN
        full = (r > mine) & (first + SPAN <= length)
        count = append(
            count,
            1,
            b * BLOCK + SPAN,
            jnp.where(full, OPEN, first),
            (r >= mine) & (first < length),
        )
    count = pad(count, 1)
    items = lax.shift_right_logical(count, 1)

    ones = jnp.ones((16, 2 * SPAN), bf16)
    lane = lax.broadcasted_iota(jnp.int32, (1, TILE), 1) & (SPAN - 1)
    row = lax.broadcasted_iota(jnp.int32, (SPAN, 1), 0)

    def keys_at(i):
        a = pl.multiple_of(addr[2 * i], 16)
        b = pl.multiple_of(addr[2 * i + 1], 16)
        return jnp.concatenate([kv[pl.ds(a, SPAN), :], kv[pl.ds(b, SPAN), :]], 0)

    def values_at(i):
        a = pl.multiple_of(addr[2 * i] + 2 * SPAN, 16)
        b = pl.multiple_of(addr[2 * i + 1] + 2 * SPAN, 16)
        both = jnp.concatenate([kv[pl.ds(a, SPAN), :], kv[pl.ds(b, SPAN), :]], 1)
        return jnp.concatenate([both, ones], 0)

    def scores(i, t, keys):
        start = pl.multiple_of(slot_of[i] * SPAN, SPAN)
        q = q_ref[pl.ds(start, SPAN), t * TILE : (t + 1) * TILE]
        return jnp.dot(keys, q, preferred_element_type=f32)

    def visit(i, cur, masked):
        slot = slot_of[i]
        values = values_at(i)
        after = jnp.minimum(i + 1, items - 1)
        keys = keys_at(after)
        if masked:
            run = jnp.where(slot == 1, LAST - mine, mine)
            limit = jnp.minimum(run * SPAN + lane, length - 1)
            spots = jnp.concatenate([base[2 * i] + row, base[2 * i + 1] + row], 0)

        def weigh(t):
            s = s_ref[cur, t]
            s_ref[1 - cur, t] = scores(after, t, keys)
            if masked:
                s = jnp.where(spots <= limit, s, HIDDEN)
            cols = slice(t * TILE, (t + 1) * TILE)
            old = m_ref[slot, :, cols]
            new = jnp.maximum(old, jnp.max(s, axis=0, keepdims=True))
            m_ref[slot, :, cols] = new
            return jnp.exp2(s * UNITS - new * UNITS).astype(bf16), jnp.exp2((old - new) * UNITS)

        def gather(t, weights, factor):
            cols = slice(t * TILE, (t + 1) * TILE)
            o_ref[slot, :, cols] = o_ref[slot, :, cols] * factor + jnp.dot(
                values, weights, preferred_element_type=f32
            )

        held = None
        for t in range(TILES):
            now = weigh(t)
            if held is not None:
                gather(t - 1, *held)
            held = now
        gather(TILES - 1, *held)

    def either(i, cur):
        masked = (base[2 * i] != OPEN) | (base[2 * i + 1] != OPEN)
        pl.when(masked)(lambda: visit(i, cur, True))
        pl.when(jnp.logical_not(masked))(lambda: visit(i, cur, False))

    keys = keys_at(0)
    for t in range(TILES):
        s_ref[0, t] = scores(0, t, keys)

    def step(i, _):
        either(2 * i, 0)
        pl.when(2 * i + 1 < items)(lambda: either(2 * i + 1, 1))
        return 0

    lax.fori_loop(0, lax.shift_right_logical(items + 1, 1), step, 0)


def scratch(sizes):
    total = sum(sizes)
    room = 3 * total + 6
    return [
        pltpu.VMEM((total * BLOCK, DEPTH), bf16),
        pltpu.SemaphoreType.DMA((len(sizes),)),
        pltpu.VMEM((2, TILES, 2 * SPAN, TILE), f32),
        pltpu.SMEM((room,), jnp.int32),
        pltpu.SMEM((room,), jnp.int32),
        pltpu.SMEM((room,), jnp.int32),
    ]


def blank(o_ref, m_ref):
    o_ref[...] = jnp.zeros_like(o_ref)
    m_ref[...] = jnp.full_like(m_ref, EMPTY)


def first_kernel(sizes, len_ref, q_ref, kv, o_ref, m_ref, s_ref, addr, base, slot_of):
    blank(o_ref, m_ref)
    work = (s_ref, addr, base, slot_of)
    attend(sizes, None, kv, len_ref, q_ref, (o_ref, m_ref), work, None)


def join_kernel(sizes, len_ref, q_ref, *refs):
    n = len(sizes)
    o_ref, m_ref, kv, sems, *work = refs[n:]
    blank(o_ref, m_ref)
    attend(sizes, refs[:n], kv, len_ref, q_ref, (o_ref, m_ref), work, sems)


def both_kernel(sizes, len_ref, theirs_ref, q_ref, *refs):
    n = len(sizes)
    _, _, _, _, o1, m1, o2, m2, kv, sems, *work = refs[n:]
    attend(sizes, refs[:n], kv, len_ref, theirs_ref, (o1, m1), work, sems)
    attend(sizes, refs[:n], kv, len_ref, q_ref, (o2, m2), work, sems, False, sizes[0])


def one_kernel(sizes, len_ref, q_ref, *refs):
    n = len(sizes)
    _, _, o_ref, m_ref, kv, sems, *work = refs[n:]
    attend(sizes, refs[:n], kv, len_ref, q_ref, (o_ref, m_ref), work, sems)


def normal(o_ref, m_ref, slot):
    total = o_ref[slot, DEPTH : DEPTH + 1, :]
    seen = total > 0.0
    safe = jnp.where(seen, total, 1.0)
    lse = jnp.where(seen, m_ref[slot] * SCALE + jnp.log(safe), HIDDEN)
    return o_ref[slot, :DEPTH, :] * (1.0 / safe), lse


def parcel_kernel(sizes, len_ref, q_ref, *refs):
    n = len(sizes)
    _, _, o_ref, m_ref, out_ref, kv, sems, *work = refs[n:]
    attend(sizes, refs[:n], kv, len_ref, q_ref, (o_ref, m_ref), work, sems)
    place = lax.broadcasted_iota(jnp.int32, (16, ROWS), 0)
    extra = jnp.zeros((16, ROWS), f32)
    for slot in range(2):
        mixed, lse = normal(o_ref, m_ref, slot)
        out_ref[slot * SPAN : (slot + 1) * SPAN, :] = mixed.astype(bf16)
        for part in range(3):
            piece = lse.astype(bf16).astype(f32)
            extra = jnp.where(place == 3 * slot + part, piece, extra)
            lse = lse - piece
    out_ref[2 * SPAN :, :] = extra.astype(bf16)


def merge_kernel(pos_ref, o_ref, m_ref, theirs_ref, out_ref, lse_ref):
    low, high, _ = low_rows(pos_ref)
    extra = theirs_ref[2 * SPAN :, :].astype(f32)
    for slot, start in enumerate((low, high)):
        mixed, lse = normal(o_ref, m_ref, slot)
        other = extra[3 * slot : 3 * slot + 1] + extra[3 * slot + 1 : 3 * slot + 2]
        other = other + extra[3 * slot + 2 : 3 * slot + 3]
        top = jnp.maximum(lse, other)
        w_own, w_other = jnp.exp(lse - top), jnp.exp(other - top)
        total = w_own + w_other
        w_own, w_other = w_own / total, w_other / total
        both = top + jnp.log(total)
        for h in range(HEADS):
            cols = slice(h * SPAN, (h + 1) * SPAN)
            block = mixed[:, cols] * w_own[:, cols] + w_other[:, cols] * theirs_ref[
                slot * SPAN : (slot + 1) * SPAN, cols
            ].astype(f32)
            out_ref[pl.ds(start, SPAN), cols] = block.T.astype(bf16)
            lse_ref[h : h + 1, pl.ds(start, SPAN)] = both[:, cols]


def cost(blocks, pairs):
    work = blocks * pairs * 2 * ROWS * SPAN
    return pl.CostEstimate(
        flops=20 * DEPTH * work, bytes_accessed=blocks * BLOCK * DEPTH * 2, transcendentals=work
    )


STATE = (
    jax.ShapeDtypeStruct((2, ACC, ROWS), f32),
    jax.ShapeDtypeStruct((2, 1, ROWS), f32),
)


def count_of(arrays):
    return tuple(a.shape[0] // BLOCK for a in arrays)


def visit(kernel, name, length, queries, blocks, given=(), shapes=STATE, pairs=None):
    sizes = count_of(blocks)
    at = 1 + len(queries) + len(blocks)
    alone = kernel is first_kernel
    spare = len(shapes) - len(given)
    shift = 0 if kernel is parcel_kernel else spare
    room = scratch(sizes)
    return pl.pallas_call(
        functools.partial(kernel, sizes),
        out_shape=shapes,
        in_specs=[SMEM] + [VMEM] * len(queries) + [VMEM if alone else ANY] * len(blocks) + [VMEM] * len(given),
        out_specs=(VMEM,) * len(shapes),
        input_output_aliases={at + i: shift + i for i in range(len(given))},
        scratch_shapes=room[2:] if alone else room,
        compiler_params=PARAMS,
        cost_estimate=cost(sum(sizes), pairs or len(queries)),
        name=name,
    )(length, *queries, *blocks, *given)


def place(y, x, z):
    return ((y % Y) * X + x % X) * Z + z % Z


def send(array, dy, dx, dz):
    pairs = [
        (place(y, x, z), place(y + dy, x + dx, z + dz))
        for y in range(Y)
        for x in range(X)
        for z in range(Z)
    ]
    return lax.ppermute(array, "ctx", pairs)


def shards(queries, keys, values, positions, valid_length):
    block = pl.pallas_call(
        pack_kv_kernel,
        out_shape=jax.ShapeDtypeStruct((BLOCK, DEPTH), bf16),
        in_specs=[SMEM, VMEM, VMEM],
        out_specs=VMEM,
        name="pack_kv",
    )(positions, keys, values)
    query, outgoing = pl.pallas_call(
        pack_q_kernel,
        out_shape=(pltpu.VMEM((QROWS, ROWS), bf16), jax.ShapeDtypeStruct((QROWS, ROWS), bf16)),
        in_specs=[SMEM, VMEM],
        out_specs=(VMEM, VMEM),
        name="pack_q",
    )(positions, queries)

    near = [block, send(block, 0, 1, 0), send(block, 0, -1, 0), send(block, 0, 2, 0)]
    far = [send(block, 0, 0, 4), send(block, 0, 0, 3), send(block, 0, 0, -3)]
    theirs = send(outgoing, 1, 0, 0)

    near, far[0] = lax.optimization_barrier((near, far[0]))
    row = jnp.concatenate(near, 0)
    up, down = send(row, 0, 0, 1), send(row, 0, 0, -1)
    own = visit(first_kernel, "first_visit", valid_length, [query], [row])
    far, own = lax.optimization_barrier((far, own))
    column = jnp.concatenate(far, 0)
    side = [send(column, 0, 1, 0), send(column, 0, -1, 0), send(column, 0, 2, 0)]
    both = [theirs, query]
    other = visit(join_kernel, "join_visit", valid_length, [theirs], [row, column])
    up2, down2 = send(up, 0, 0, 1), send(down, 0, 0, -1)
    state = visit(
        both_kernel, "both_visit", valid_length, both, [up, down], (*other, *own), STATE + STATE
    )
    other = visit(one_kernel, "side_visit", valid_length, [theirs], side, state[:2])
    late = [up2, down2]
    packet = jax.ShapeDtypeStruct((QROWS, ROWS), bf16)
    parcel = visit(
        parcel_kernel, "parcel_visit", valid_length, [theirs], late, other, STATE + (packet,)
    )[2]
    back = send(parcel, 1, 0, 0)
    own, own_max = visit(one_kernel, "own_visit", valid_length, [query], [column, up] + side + late, state[2:])
    return pl.pallas_call(
        merge_kernel,
        out_shape=(
            jax.ShapeDtypeStruct((2 * SPAN, ROWS), bf16),
            jax.ShapeDtypeStruct((HEADS, 2 * SPAN), f32),
        ),
        in_specs=[SMEM, VMEM, VMEM, VMEM],
        out_specs=(VMEM, VMEM),
        compiler_params=PARAMS,
        name="merge",
    )(positions, own, own_max, back)


def solution(mesh):
    placed = (
        P(("dp", "ctx"), None),
        P(("dp", "ctx"), None),
        P(("dp", "ctx"), None),
        P(("dp", "ctx")),
        P("dp"),
    )
    return jax.shard_map(
        shards,
        mesh=mesh,
        in_specs=placed,
        out_specs=(P(("dp", "ctx"), None), P(None, ("dp", "ctx"))),
        check_vma=False,
    )
```

```python
import functools
import math

import jax
import jax.numpy as jnp
from jax import lax
from jax.experimental import pallas as pl
from jax.experimental.pallas import tpu as pltpu
from jax.sharding import PartitionSpec as P

SPAN = 128
HEADS = 8
DEPTH = 128
ROWS = HEADS * SPAN
BLOCK = 4 * SPAN + 16
QROWS = 2 * SPAN + 16
ACC = DEPTH + 16
TILE = 256
TILES = ROWS // TILE
LAST = 127
UNITS = math.log2(math.e) / math.sqrt(DEPTH)
SCALE = 1.0 / math.sqrt(DEPTH)
EMPTY = -1e20
HIDDEN = -1e30
OPEN = -(1 << 20)
SHUT = 1 << 20
Y, X, Z = 2, 4, 8

f32 = jnp.float32
bf16 = jnp.bfloat16
VMEM = pl.BlockSpec(memory_space=pltpu.VMEM)
SMEM = pl.BlockSpec(memory_space=pltpu.SMEM)
ANY = pl.BlockSpec(memory_space=pl.ANY)
PARAMS = pltpu.CompilerParams(vmem_limit_bytes=48 * 2**20)


def low_rows(pos_ref):
    first, second = pos_ref[0], pos_ref[SPAN]
    return (
        pl.multiple_of(jnp.where(first < second, 0, SPAN), SPAN),
        pl.multiple_of(jnp.where(first < second, SPAN, 0), SPAN),
        lax.shift_right_logical(jnp.minimum(first, second), 7),
    )


def pack_kv_kernel(pos_ref, k_ref, v_ref, out_ref):
    low, high, run = low_rows(pos_ref)
    for i, start in enumerate((low, high)):
        out_ref[i * SPAN : (i + 1) * SPAN, :] = k_ref[pl.ds(start, SPAN), :]
        out_ref[(2 + i) * SPAN : (3 + i) * SPAN, :] = v_ref[pl.ds(start, SPAN), :].T
    out_ref[4 * SPAN :, :] = jnp.full((16, DEPTH), run.astype(f32), f32).astype(bf16)


def pack_q_kernel(pos_ref, q_ref, out_ref, copy_ref):
    low, high, run = low_rows(pos_ref)
    for i, start in enumerate((low, high)):
        for h in range(HEADS):
            cols = slice(h * SPAN, (h + 1) * SPAN)
            out_ref[i * SPAN : (i + 1) * SPAN, cols] = q_ref[pl.ds(start, SPAN), cols].T
    out_ref[2 * SPAN :, :] = jnp.full((16, ROWS), run.astype(f32), f32).astype(bf16)
    copy_ref[...] = out_ref[...]


def run_of(tile):
    return jnp.max(tile.astype(f32)).astype(jnp.int32)


def attend(sizes, kv_refs, kv, len_ref, q_ref, state, work, sems, fetch=True, since=0):
    o_ref, m_ref = state
    s_ref, addr, base, slot_of = work
    total = sum(sizes)
    if fetch and kv_refs is not None:
        copies = []
        at = 0
        for i, (ref, blocks) in enumerate(zip(kv_refs, sizes)):
            copies.append(
                pltpu.make_async_copy(ref, kv.at[pl.ds(at * BLOCK, blocks * BLOCK)], sems.at[i])
            )
            at += blocks
        for c in copies:
            c.start()
        for c in copies:
            c.wait()

    length = len_ref[0]
    mine = run_of(q_ref[2 * SPAN : 2 * SPAN + 16, :DEPTH])
    seen = range(since, total)
    runs = {b: run_of(kv[b * BLOCK + 4 * SPAN : (b + 1) * BLOCK, :]) for b in seen}

    def append(count, slot, row, first, wanted):
        addr[count] = row
        base[count] = first
        slot_of[lax.shift_right_logical(count, 1)] = slot
        return count + wanted.astype(jnp.int32)

    def pad(count, slot):
        return append(count, slot, since * BLOCK, SHUT, (count & 1) == 1)

    count = jnp.int32(0)
    for b in seen:
        r = runs[b]
        count = append(count, 0, b * BLOCK, jnp.where(r < mine, OPEN, r * SPAN), r <= mine)
    count = pad(count, 0)
    for b in seen:
        count = append(count, 1, b * BLOCK, OPEN, jnp.bool_(True))
    for b in seen:
        r = runs[b]
        first = (LAST - r) * SPAN
        full = (r > mine) & (first + SPAN <= length)
        count = append(
            count,
            1,
            b * BLOCK + SPAN,
            jnp.where(full, OPEN, first),
            (r >= mine) & (first < length),
        )
    count = pad(count, 1)
    items = lax.shift_right_logical(count, 1)

    ones = jnp.ones((16, 2 * SPAN), bf16)
    lane = lax.broadcasted_iota(jnp.int32, (1, TILE), 1) & (SPAN - 1)
    row = lax.broadcasted_iota(jnp.int32, (SPAN, 1), 0)

    def keys_at(i):
        a = pl.multiple_of(addr[2 * i], 16)
        b = pl.multiple_of(addr[2 * i + 1], 16)
        return jnp.concatenate([kv[pl.ds(a, SPAN), :], kv[pl.ds(b, SPAN), :]], 0)

    def values_at(i):
        a = pl.multiple_of(addr[2 * i] + 2 * SPAN, 16)
        b = pl.multiple_of(addr[2 * i + 1] + 2 * SPAN, 16)
        both = jnp.concatenate([kv[pl.ds(a, SPAN), :], kv[pl.ds(b, SPAN), :]], 1)
        return jnp.concatenate([both, ones], 0)

    def scores(i, t, keys):
        start = pl.multiple_of(slot_of[i] * SPAN, SPAN)
        q = q_ref[pl.ds(start, SPAN), t * TILE : (t + 1) * TILE]
        return jnp.dot(keys, q, preferred_element_type=f32)

    def visit(i, cur, masked):
        slot = slot_of[i]
        values = values_at(i)
        after = jnp.minimum(i + 1, items - 1)
        keys = keys_at(after)
        if masked:
            run = jnp.where(slot == 1, LAST - mine, mine)
            limit = jnp.minimum(run * SPAN + lane, length - 1)
            spots = jnp.concatenate([base[2 * i] + row, base[2 * i + 1] + row], 0)

        def weigh(t):
            s = s_ref[cur, t]
            s_ref[1 - cur, t] = scores(after, t, keys)
            if masked:
                s = jnp.where(spots <= limit, s, HIDDEN)
            cols = slice(t * TILE, (t + 1) * TILE)
            old = m_ref[slot, :, cols]
            new = jnp.maximum(old, jnp.max(s, axis=0, keepdims=True))
            m_ref[slot, :, cols] = new
            return jnp.exp2(s * UNITS - new * UNITS).astype(bf16), jnp.exp2((old - new) * UNITS)

        def gather(t, weights, factor):
            cols = slice(t * TILE, (t + 1) * TILE)
            o_ref[slot, :, cols] = o_ref[slot, :, cols] * factor + jnp.dot(
                values, weights, preferred_element_type=f32
            )

        held = None
        for t in range(TILES):
            now = weigh(t)
            if held is not None:
                gather(t - 1, *held)
            held = now
        gather(TILES - 1, *held)

    def either(i, cur):
        masked = (base[2 * i] != OPEN) | (base[2 * i + 1] != OPEN)
        pl.when(masked)(lambda: visit(i, cur, True))
        pl.when(jnp.logical_not(masked))(lambda: visit(i, cur, False))

    keys = keys_at(0)
    for t in range(TILES):
        s_ref[0, t] = scores(0, t, keys)

    def step(i, _):
        either(2 * i, 0)
        pl.when(2 * i + 1 < items)(lambda: either(2 * i + 1, 1))
        return 0

    lax.fori_loop(0, lax.shift_right_logical(items + 1, 1), step, 0)


def scratch(sizes):
    total = sum(sizes)
    room = 3 * total + 6
    return [
        pltpu.VMEM((total * BLOCK, DEPTH), bf16),
        pltpu.SemaphoreType.DMA((len(sizes),)),
        pltpu.VMEM((2, TILES, 2 * SPAN, TILE), f32),
        pltpu.SMEM((room,), jnp.int32),
        pltpu.SMEM((room,), jnp.int32),
        pltpu.SMEM((room,), jnp.int32),
    ]


def blank(o_ref, m_ref):
    o_ref[...] = jnp.zeros_like(o_ref)
    m_ref[...] = jnp.full_like(m_ref, EMPTY)


def first_kernel(sizes, len_ref, q_ref, kv, o_ref, m_ref, s_ref, addr, base, slot_of):
    blank(o_ref, m_ref)
    work = (s_ref, addr, base, slot_of)
    attend(sizes, None, kv, len_ref, q_ref, (o_ref, m_ref), work, None)


def join_kernel(sizes, len_ref, theirs_ref, q_ref, *refs):
    n = len(sizes)
    _, _, o1, m1, o2, m2, kv, sems, *work = refs[n:]
    blank(o1, m1)
    attend(sizes, refs[:n], kv, len_ref, theirs_ref, (o1, m1), work, sems)
    attend(sizes, refs[:n], kv, len_ref, q_ref, (o2, m2), work, sems, False, sizes[0])


def both_kernel(sizes, len_ref, theirs_ref, q_ref, *refs):
    n = len(sizes)
    _, _, _, _, o1, m1, o2, m2, kv, sems, *work = refs[n:]
    attend(sizes, refs[:n], kv, len_ref, theirs_ref, (o1, m1), work, sems)
    attend(sizes, refs[:n], kv, len_ref, q_ref, (o2, m2), work, sems, False, sizes[0])


def one_kernel(sizes, len_ref, q_ref, *refs):
    n = len(sizes)
    _, _, o_ref, m_ref, kv, sems, *work = refs[n:]
    attend(sizes, refs[:n], kv, len_ref, q_ref, (o_ref, m_ref), work, sems)


def normal(o_ref, m_ref, slot):
    total = o_ref[slot, DEPTH : DEPTH + 1, :]
    seen = total > 0.0
    safe = jnp.where(seen, total, 1.0)
    lse = jnp.where(seen, m_ref[slot] * SCALE + jnp.log(safe), HIDDEN)
    return o_ref[slot, :DEPTH, :] * (1.0 / safe), lse


def parcel_kernel(sizes, len_ref, q_ref, *refs):
    n = len(sizes)
    _, _, o_ref, m_ref, out_ref, kv, sems, *work = refs[n:]
    attend(sizes, refs[:n], kv, len_ref, q_ref, (o_ref, m_ref), work, sems)
    place = lax.broadcasted_iota(jnp.int32, (16, ROWS), 0)
    extra = jnp.zeros((16, ROWS), f32)
    for slot in range(2):
        mixed, lse = normal(o_ref, m_ref, slot)
        out_ref[slot * SPAN : (slot + 1) * SPAN, :] = mixed.astype(bf16)
        for part in range(3):
            piece = lse.astype(bf16).astype(f32)
            extra = jnp.where(place == 3 * slot + part, piece, extra)
            lse = lse - piece
    out_ref[2 * SPAN :, :] = extra.astype(bf16)


def merge_kernel(pos_ref, o_ref, m_ref, theirs_ref, out_ref, lse_ref):
    low, high, _ = low_rows(pos_ref)
    extra = theirs_ref[2 * SPAN :, :].astype(f32)
    for slot, start in enumerate((low, high)):
        mixed, lse = normal(o_ref, m_ref, slot)
        other = extra[3 * slot : 3 * slot + 1] + extra[3 * slot + 1 : 3 * slot + 2]
        other = other + extra[3 * slot + 2 : 3 * slot + 3]
        top = jnp.maximum(lse, other)
        w_own, w_other = jnp.exp(lse - top), jnp.exp(other - top)
        total = w_own + w_other
        w_own, w_other = w_own / total, w_other / total
        both = top + jnp.log(total)
        for h in range(HEADS):
            cols = slice(h * SPAN, (h + 1) * SPAN)
            block = mixed[:, cols] * w_own[:, cols] + w_other[:, cols] * theirs_ref[
                slot * SPAN : (slot + 1) * SPAN, cols
            ].astype(f32)
            out_ref[pl.ds(start, SPAN), cols] = block.T.astype(bf16)
            lse_ref[h : h + 1, pl.ds(start, SPAN)] = both[:, cols]


def cost(blocks, pairs):
    work = blocks * pairs * 2 * ROWS * SPAN
    return pl.CostEstimate(
        flops=20 * DEPTH * work, bytes_accessed=blocks * BLOCK * DEPTH * 2, transcendentals=work
    )


STATE = (
    jax.ShapeDtypeStruct((2, ACC, ROWS), f32),
    jax.ShapeDtypeStruct((2, 1, ROWS), f32),
)


def count_of(arrays):
    return tuple(a.shape[0] // BLOCK for a in arrays)


def visit(kernel, name, length, queries, blocks, given=(), shapes=STATE, pairs=None):
    sizes = count_of(blocks)
    at = 1 + len(queries) + len(blocks)
    alone = kernel is first_kernel
    spare = len(shapes) - len(given)
    shift = 0 if kernel is parcel_kernel else spare
    room = scratch(sizes)
    return pl.pallas_call(
        functools.partial(kernel, sizes),
        out_shape=shapes,
        in_specs=[SMEM] + [VMEM] * len(queries) + [VMEM if alone else ANY] * len(blocks) + [VMEM] * len(given),
        out_specs=(VMEM,) * len(shapes),
        input_output_aliases={at + i: shift + i for i in range(len(given))},
        scratch_shapes=room[2:] if alone else room,
        compiler_params=PARAMS,
        cost_estimate=cost(sum(sizes), pairs or len(queries)),
        name=name,
    )(length, *queries, *blocks, *given)


def place(y, x, z):
    return ((y % Y) * X + x % X) * Z + z % Z


def send(array, dy, dx, dz):
    pairs = [
        (place(y, x, z), place(y + dy, x + dx, z + dz))
        for y in range(Y)
        for x in range(X)
        for z in range(Z)
    ]
    return lax.ppermute(array, "ctx", pairs)


def shards(queries, keys, values, positions, valid_length):
    block = pl.pallas_call(
        pack_kv_kernel,
        out_shape=jax.ShapeDtypeStruct((BLOCK, DEPTH), bf16),
        in_specs=[SMEM, VMEM, VMEM],
        out_specs=VMEM,
        name="pack_kv",
    )(positions, keys, values)
    query, outgoing = pl.pallas_call(
        pack_q_kernel,
        out_shape=(pltpu.VMEM((QROWS, ROWS), bf16), jax.ShapeDtypeStruct((QROWS, ROWS), bf16)),
        in_specs=[SMEM, VMEM],
        out_specs=(VMEM, VMEM),
        name="pack_q",
    )(positions, queries)

    near = [block, send(block, 0, 1, 0), send(block, 0, -1, 0), send(block, 0, 2, 0)]
    far = [send(block, 0, 0, 4), send(block, 0, 0, 3), send(block, 0, 0, -3)]
    theirs = send(outgoing, 1, 0, 0)

    near, far[0] = lax.optimization_barrier((near, far[0]))
    row = jnp.concatenate(near, 0)
    up, down = send(row, 0, 0, 1), send(row, 0, 0, -1)
    own = visit(first_kernel, "first_visit", valid_length, [query], [row])
    far, own = lax.optimization_barrier((far, own))
    column = jnp.concatenate(far, 0)
    side = [send(column, 0, 1, 0), send(column, 0, -1, 0), send(column, 0, 2, 0)]
    both = [theirs, query]
    state = visit(
        join_kernel, "join_visit", valid_length, both, [row, column], tuple(own), STATE + STATE
    )
    up2, down2 = send(up, 0, 0, 1), send(down, 0, 0, -1)
    state = visit(
        both_kernel, "both_visit", valid_length, both, [up, down], state, STATE + STATE
    )
    other = visit(one_kernel, "side_visit", valid_length, [theirs], side, state[:2])
    late = [up2, down2]
    packet = jax.ShapeDtypeStruct((QROWS, ROWS), bf16)
    parcel = visit(
        parcel_kernel, "parcel_visit", valid_length, [theirs], late, other, STATE + (packet,)
    )[2]
    back = send(parcel, 1, 0, 0)
    own, own_max = visit(one_kernel, "own_visit", valid_length, [query], [up] + side + late, state[2:])
    return pl.pallas_call(
        merge_kernel,
        out_shape=(
            jax.ShapeDtypeStruct((2 * SPAN, ROWS), bf16),
            jax.ShapeDtypeStruct((HEADS, 2 * SPAN), f32),
        ),
        in_specs=[SMEM, VMEM, VMEM, VMEM],
        out_specs=(VMEM, VMEM),
        compiler_params=PARAMS,
        name="merge",
    )(positions, own, own_max, back)


def solution(mesh):
    placed = (
        P(("dp", "ctx"), None),
        P(("dp", "ctx"), None),
        P(("dp", "ctx"), None),
        P(("dp", "ctx")),
        P("dp"),
    )
    return jax.shard_map(
        shards,
        mesh=mesh,
        in_specs=placed,
        out_specs=(P(("dp", "ctx"), None), P(None, ("dp", "ctx"))),
        check_vma=False,
    )
```
